32 devices in a mesh: groups: 2 (over x), centers: 16 (over z, y, core).
Axes of the slice: x: 2, y: 2, z: 4, core: 2. Of those that a mesh axis runs over, the one named last changes fastest.
Arguments:
- center_feats: bfloat16 [32768, 1024], P(('groups', 'centers')), parts along dimension 0, may hold values from -8 to 8
- coeffs: bfloat16 [32768, 1000], P(('groups', 'centers')), parts along dimension 0, may hold values from -0.119628906 to 0.119628906
- labels: bfloat16 [256, 1000], P(('groups', 'centers')), parts along dimension 0, may hold values from -6 to 6
- running: float32 [256, 1000], P(('groups', 'centers')), parts along dimension 0, may hold values from -6 to 6
- batch_index: int32 [256], P(('groups', 'centers')), parts along dimension 0, may hold values from 0 to 16383, as said below
- landmark_index: int32 [4096], P(('groups', 'centers')), parts along dimension 0, may hold values from 0 to 16383, as said below
Outputs:
- new_running: float32 [256, 1000], P(('groups', 'centers')), parts along dimension 0
- projection: float32 [4096, 1000], P(('groups', 'centers')), parts along dimension 0
The draws below stay inside these ranges and needn't reach their ends.
There are 2 independent parts, one for each index of `groups`. The reference program is written for one: setup_inputs(seed, part) draws one part's arguments, and reference() takes and returns one part's arrays. A program takes and returns all parts, laid end to end along the dimension named above; each array names one. Nothing has to cross between parts.
Inputs may be any that keep to these rules, and one draw needn't show every extreme that they name: The entries of batch_index in rows j * 8 to (j + 1) * 8 - 1 are distinct and lie in j * 1024 to (j + 1) * 1024 - 1. The entries of landmark_index in rows j * 128 to (j + 1) * 128 - 1 are distinct and lie in j * 1024 to (j + 1) * 1024 - 1.
All inputs are finite; a program needn't handle non-finite values.
Results may differ from the reference program's by a relative error of at most 0.002.
Values may be sent and summed in bfloat16 or wider, within the bound.
No kernel may reach another device: no remote copies, remote signals or barrier semaphores. Data moves between devices by JAX's collectives and lax.ppermute only.
A program may use at most 64 MiB of HBM per device.

```python
import math
import jax
import jax.numpy as jnp
from jax import lax

D = 1024
OUT = 1000
CEN_DEV = 1024
B_DEV = 8
L_DEV = 128
POOL = 16384
BATCH = 128
LANDMARKS = 2048


def slab_picks(key, per_block, blocks):
    keys = jax.random.split(key, blocks)
    picks = jax.vmap(lambda one: jax.random.permutation(one, CEN_DEV)[:per_block])(keys)
    offsets = jnp.arange(blocks, dtype=jnp.int32)[:, None] * CEN_DEV
    return (picks.astype(jnp.int32) + offsets).reshape(-1)


def draw_batch_index(key, part):
    return slab_picks(jax.random.fold_in(key, 11), B_DEV, BATCH // B_DEV)


def draw_landmark_index(key, part):
    return slab_picks(jax.random.fold_in(key, 23), L_DEV, LANDMARKS // L_DEV)


def draw_center_feats(key, part):
    member = jax.random.randint(jax.random.fold_in(key, 3), (POOL,), 0, OUT)
    low_scale = 0.5
    high_scale = 1.5
    log_scale = jax.random.uniform(jax.random.fold_in(key, 5), (OUT, 1), jnp.float32, math.log(low_scale), math.log(high_scale))
    means = jax.random.truncated_normal(jax.random.fold_in(key, 7), -3.0, 3.0, (OUT, D), jnp.float32) * jnp.exp(log_scale)
    log_spread = jax.random.uniform(jax.random.fold_in(key, 9), (POOL, 1), jnp.float32, math.log(0.5), math.log(1.0))
    noise = jax.random.truncated_normal(jax.random.fold_in(key, 13), -3.0, 3.0, (POOL, D), jnp.float32)
    feats = jnp.take(means, member, axis=0) + jnp.exp(log_spread) * noise
    return feats.astype(jnp.bfloat16)


def block_scale(own_key, shape, pieces, low, largest):
    gain, own = 1.0, jax.random.fold_in(own_key, 6)
    for position, shards_of in pieces:
        draws = jnp.exp(jax.random.uniform(jax.random.fold_in(own, position), (shards_of,), jnp.float32, low / len(pieces), largest / len(pieces)))
        gain = gain * jnp.repeat(draws, shape[position] // shards_of).reshape([-1 if axis == position else 1 for axis in range(len(shape))])
    return gain


def normal_values(rng, shape, spread, limit, shards=(), held_as=jnp.bfloat16):
    factor_of = block_scale(rng, shape, shards, -0.22, 0.18) if shards else 1.0
    drawn = jax.random.normal(rng, shape, jnp.float32) * spread * factor_of
    return jnp.minimum(jnp.maximum(drawn, -limit), limit).astype(held_as)


def setup_inputs(seed: int = 0, part: int = 0) -> dict:
    arg_keys = jax.random.split(jax.random.key(seed), 7)
    own_keys = jax.random.split(jax.random.fold_in(arg_keys[6], part), 7)
    center_feats = draw_center_feats(jax.random.fold_in(jax.random.fold_in(arg_keys[6], part), 71), part)
    coeffs = normal_values(own_keys[1], (POOL, OUT), 0.02, 0.119628906, ((0, 16),))
    labels = normal_values(own_keys[2], (BATCH, OUT), 1.0, 6.0, ((0, 16),))
    running = normal_values(own_keys[3], (BATCH, OUT), 1.0, 6.0, ((0, 16),), jnp.float32)
    batch_index = draw_batch_index(jax.random.fold_in(jax.random.fold_in(arg_keys[6], part), 71), part)
    landmark_index = draw_landmark_index(jax.random.fold_in(jax.random.fold_in(arg_keys[6], part), 71), part)
    return {"center_feats": center_feats, "coeffs": coeffs, "labels": labels, "running": running, "batch_index": batch_index, "landmark_index": landmark_index}


def kernel_tile(row_feats, col_feats):
    row_norms = jnp.sum(row_feats.astype(jnp.float32) ** 2, axis=-1)
    col_norms = jnp.sum(col_feats.astype(jnp.float32) ** 2, axis=-1)
    cross = jnp.dot(row_feats, col_feats.T, preferred_element_type=jnp.float32)
    dist = row_norms[:, None] + col_norms[None, :] - 2.0 * cross
    return jnp.exp(-dist / D).astype(jnp.bfloat16)


def reference(center_feats, coeffs, labels, running, batch_index, landmark_index):
    batch_feats = jnp.take(center_feats, batch_index, axis=0)

    def add_block(total, block):
        start = (block * CEN_DEV).astype(jnp.int32)
        feats = lax.dynamic_slice_in_dim(center_feats, start, CEN_DEV, 0)
        weights = lax.dynamic_slice_in_dim(coeffs, start, CEN_DEV, 0)
        tile = kernel_tile(batch_feats, feats)
        return total + jnp.dot(tile, weights, preferred_element_type=jnp.float32), None

    blocks = POOL // CEN_DEV
    pred, unused = lax.scan(add_block, jnp.zeros((BATCH, OUT), jnp.float32), jnp.arange(blocks, dtype=jnp.int32))
    new_running = running + pred
    resid = (new_running - labels.astype(jnp.float32)).astype(jnp.bfloat16)
    land_feats = jnp.take(center_feats, landmark_index, axis=0)
    projection = jnp.dot(kernel_tile(land_feats, batch_feats), resid, preferred_element_type=jnp.float32)
    return new_running, projection
```

```python
import functools

import jax
import jax.numpy as jnp
from jax import lax
from jax.experimental import pallas as pl
from jax.experimental.pallas import tpu as pltpu
from jax.sharding import PartitionSpec as P

SCALE = 1024.0
VMEM_LIMIT = 48 * 1024 * 1024


def gather_kernel(index_ref, feats_ref, out_ref, blocks, rows_out, sems):
    picks = index_ref.shape[0]
    slab = feats_ref.shape[0]
    copies = []
    for i in range(picks):
        row = lax.rem(index_ref[i], slab)
        start = pl.multiple_of((row // 16) * 16, 16)
        copy = pltpu.make_async_copy(
            feats_ref.at[pl.ds(start, 16), :], blocks.at[i], sems.at[i]
        )
        copy.start()
        copies.append(copy)
    for i in range(picks):
        copies[i].wait()
        inside = lax.rem(index_ref[i], 16)
        block = blocks[i].astype(jnp.float32)
        here = lax.broadcasted_iota(jnp.int32, block.shape, 0) == inside
        rows_out[i : i + 1, :] = jnp.sum(
            jnp.where(here, block, 0.0), axis=0, keepdims=True
        )
    rows = rows_out[...].astype(out_ref.dtype)
    for chip in range(out_ref.shape[0]):
        out_ref[chip] = rows


def gather_rows(center_feats, batch_index, chips):
    picks, width = batch_index.shape[0], center_feats.shape[1]
    return pl.pallas_call(
        gather_kernel,
        out_shape=jax.ShapeDtypeStruct((chips, picks, width), center_feats.dtype),
        in_specs=[
            pl.BlockSpec(memory_space=pltpu.SMEM),
            pl.BlockSpec(memory_space=pltpu.HBM),
        ],
        out_specs=pl.BlockSpec(memory_space=pltpu.VMEM),
        scratch_shapes=[
            pltpu.VMEM((picks, 16, width), center_feats.dtype),
            pltpu.VMEM((picks, width), jnp.float32),
            pltpu.SemaphoreType.DMA((picks,)),
        ],
        compiler_params=pltpu.CompilerParams(vmem_limit_bytes=VMEM_LIMIT),
    )(batch_index, center_feats)


def nt(a, b):
    return lax.dot_general(
        a, b, (((1,), (1,)), ((), ())), preferred_element_type=jnp.float32
    )


def tile_kernel(mine_ref, other_ref, feats_ref, coeffs_ref, land_ref,
                pred_mine_ref, pred_other_ref, land_tile_ref):
    slab = feats_ref.shape[0]
    half = mine_ref.shape[0]
    batch = jnp.concatenate([mine_ref[...], other_ref[...]], axis=0)
    feats = feats_ref[...]
    wide = feats.astype(jnp.float32)
    center_norms = jnp.sum(wide * wide, axis=1, keepdims=True)
    batch_wide = batch.astype(jnp.float32)
    batch_norms = jnp.sum(batch_wide * batch_wide, axis=1, keepdims=True)
    cross = nt(feats, batch)
    dist = center_norms + batch_norms.T - 2.0 * cross
    tile = jnp.exp(-dist / SCALE).astype(jnp.bfloat16)
    spread = jnp.dot(coeffs_ref[...], tile, preferred_element_type=jnp.float32)
    pred = spread.T
    pred_mine_ref[...] = pred[:half]
    pred_other_ref[...] = pred[half:]
    local = lax.rem(land_ref[...], slab)
    lands = local.shape[0]
    chosen = lax.broadcasted_iota(jnp.int32, (lands, slab), 1) == local
    pick = jnp.where(chosen, 1.0, 0.0).astype(jnp.bfloat16)
    land_tile_ref[...] = jnp.dot(
        pick, tile, preferred_element_type=jnp.float32
    ).astype(jnp.bfloat16)


def tile_and_pred(mine, other, center_feats, coeffs_t, landmark_index):
    half, lands, out = mine.shape[0], landmark_index.shape[0], coeffs_t.shape[0]
    slab, width = center_feats.shape
    vmem = pl.BlockSpec(memory_space=pltpu.VMEM)
    return pl.pallas_call(
        tile_kernel,
        out_shape=(
            jax.ShapeDtypeStruct((half, out), jnp.float32),
            jax.ShapeDtypeStruct((half, out), jnp.float32),
            jax.ShapeDtypeStruct((lands, 2 * half), jnp.bfloat16),
        ),
        in_specs=[vmem] * 5,
        out_specs=(vmem,) * 3,
        compiler_params=pltpu.CompilerParams(vmem_limit_bytes=VMEM_LIMIT),
    )(mine, other, center_feats, coeffs_t, landmark_index.reshape(lands, 1))


def resid_kernel(parts_ref, running_ref, labels_ref, new_ref, resid_ref):
    total = running_ref[...]
    for chip in range(parts_ref.shape[0]):
        total = total + parts_ref[chip]
    new_ref[...] = total
    resid = (total - labels_ref[...].astype(jnp.float32)).astype(jnp.bfloat16)
    for chip in range(resid_ref.shape[0]):
        resid_ref[chip] = resid


def residuals(parts, running, labels):
    chips, rows, out = parts.shape
    vmem = pl.BlockSpec(memory_space=pltpu.VMEM)
    return pl.pallas_call(
        resid_kernel,
        out_shape=(
            jax.ShapeDtypeStruct((rows, out), jnp.float32),
            jax.ShapeDtypeStruct((chips, rows, out), jnp.bfloat16),
        ),
        in_specs=[vmem] * 3,
        out_specs=(vmem,) * 2,
        compiler_params=pltpu.CompilerParams(vmem_limit_bytes=VMEM_LIMIT),
    )(parts, running, labels)


def per_device(size, center_feats, coeffs, labels, running, batch_index, landmark_index):
    chips = size // 2
    swap = [(i, i ^ 1) for i in range(size)]
    across = [[core + 2 * chip for chip in range(chips)] for core in range(2)]

    def exchange(blocks):
        return lax.all_to_all(
            blocks, "centers", 0, 0, axis_index_groups=across, tiled=True
        )

    picks = batch_index.shape[0]
    own = gather_rows(center_feats, batch_index, chips)
    mine = exchange(own).reshape(chips * picks, -1)
    other = lax.ppermute(mine, "centers", swap)
    pred_mine, pred_other, land_tile = tile_and_pred(
        mine, other, center_feats, coeffs.T, landmark_index
    )
    pair = pred_mine + lax.ppermute(pred_other, "centers", swap)
    parts = exchange(pair.reshape(chips, picks, -1))
    new_running, resid = residuals(parts, running, labels)
    resid_mine = exchange(resid).reshape(chips * picks, -1)
    resid_other = lax.ppermute(resid_mine, "centers", swap)
    projection = jnp.dot(
        land_tile,
        jnp.concatenate([resid_mine, resid_other], axis=0),
        preferred_element_type=jnp.float32,
    )
    return (new_running, projection)


def solution(mesh):
    row = P(("groups", "centers"), None)
    flat = P(("groups", "centers"))
    return jax.shard_map(
        functools.partial(per_device, mesh.shape["centers"]),
        mesh=mesh,
        in_specs=(row, row, row, row, flat, flat),
        out_specs=(row, row),
        check_vma=False,
    )
```

```python
import functools

import jax
import jax.numpy as jnp
from jax import lax
from jax.experimental import pallas as pl
from jax.experimental.pallas import tpu as pltpu
from jax.sharding import PartitionSpec as P

SCALE = 1024.0
VMEM_LIMIT = 16 * 1024 * 1024


def gather_kernel(index_ref, feats_ref, out_ref, rows):
    for i in range(index_ref.shape[0]):
        row = index_ref[i]
        start = pl.multiple_of((row // 16) * 16, 16)
        block = feats_ref[pl.ds(start, 16), :].astype(jnp.float32)
        here = lax.broadcasted_iota(jnp.int32, block.shape, 0) == row - start
        rows[i : i + 1, :] = jnp.sum(jnp.where(here, block, 0.0), axis=0, keepdims=True)
    picked = rows[...].astype(out_ref.dtype)
    for chip in range(out_ref.shape[0]):
        out_ref[chip] = picked


def gather_rows(center_feats, batch_index, chips):
    picks, width = batch_index.shape[0], center_feats.shape[1]
    vmem = pl.BlockSpec(memory_space=pltpu.VMEM)
    return pl.pallas_call(
        gather_kernel,
        out_shape=jax.ShapeDtypeStruct((chips, picks, width), center_feats.dtype),
        in_specs=[pl.BlockSpec(memory_space=pltpu.SMEM), vmem],
        out_specs=vmem,
        scratch_shapes=[pltpu.VMEM((picks, width), jnp.float32)],
        compiler_params=pltpu.CompilerParams(vmem_limit_bytes=VMEM_LIMIT),
    )(batch_index, center_feats)


def nt(a, b):
    return lax.dot_general(
        a, b, (((1,), (1,)), ((), ())), preferred_element_type=jnp.float32
    )


def tile_kernel(mine_ref, other_ref, feats_ref, land_ref, tile_ref, land_tile_ref):
    slab = feats_ref.shape[0]
    batch = jnp.concatenate([mine_ref[...], other_ref[...]], axis=0)
    feats = feats_ref[...]
    wide = feats.astype(jnp.float32)
    center_norms = jnp.sum(wide * wide, axis=1, keepdims=True)
    batch_wide = batch.astype(jnp.float32)
    batch_norms = jnp.sum(batch_wide * batch_wide, axis=1, keepdims=True)
    dist = center_norms + batch_norms.T - 2.0 * nt(feats, batch)
    tile = jnp.exp(-dist / SCALE).astype(jnp.bfloat16)
    tile_ref[...] = tile
    local = land_ref[...]
    chosen = lax.broadcasted_iota(jnp.int32, (local.shape[0], slab), 1) == local
    pick = jnp.where(chosen, 1.0, 0.0).astype(jnp.bfloat16)
    land_tile_ref[...] = jnp.dot(
        pick, tile, preferred_element_type=jnp.float32
    ).astype(jnp.bfloat16)


def kernel_tiles(mine, other, center_feats, land_local):
    half, lands, slab = mine.shape[0], land_local.shape[0], center_feats.shape[0]
    vmem = pl.BlockSpec(memory_space=pltpu.VMEM)
    return pl.pallas_call(
        tile_kernel,
        out_shape=(
            jax.ShapeDtypeStruct((slab, 2 * half), jnp.bfloat16),
            jax.ShapeDtypeStruct((lands, 2 * half), jnp.bfloat16),
        ),
        in_specs=[vmem] * 4,
        out_specs=(vmem,) * 2,
        compiler_params=pltpu.CompilerParams(
            vmem_limit_bytes=VMEM_LIMIT * (1 if half <= 64 else 3)
        ),
    )(mine, other, center_feats, land_local.reshape(lands, 1))


def pred_kernel(tile_ref, coeffs_ref, mine_ref, other_ref):
    pred = jnp.dot(
        coeffs_ref[...], tile_ref[...], preferred_element_type=jnp.float32
    ).T
    half = mine_ref.shape[0]
    mine_ref[...] = pred[:half]
    other_ref[...] = pred[half:]


def predictions(tile, coeffs_t):
    half, out = tile.shape[1] // 2, coeffs_t.shape[0]
    vmem = pl.BlockSpec(memory_space=pltpu.VMEM)
    return pl.pallas_call(
        pred_kernel,
        out_shape=(jax.ShapeDtypeStruct((half, out), jnp.float32),) * 2,
        in_specs=[vmem] * 2,
        out_specs=(vmem,) * 2,
        compiler_params=pltpu.CompilerParams(
            vmem_limit_bytes=VMEM_LIMIT * (1 if half <= 64 else 3)
        ),
    )(tile, coeffs_t)


def resid_kernel(parts_ref, running_ref, labels_ref, new_ref, resid_ref):
    total = running_ref[...]
    for chip in range(parts_ref.shape[0]):
        total = total + parts_ref[chip]
    new_ref[...] = total
    resid = (total - labels_ref[...].astype(jnp.float32)).astype(jnp.bfloat16)
    for chip in range(resid_ref.shape[0]):
        resid_ref[chip] = resid


def residuals(parts, running, labels):
    chips, rows, out = parts.shape
    vmem = pl.BlockSpec(memory_space=pltpu.VMEM)
    return pl.pallas_call(
        resid_kernel,
        out_shape=(
            jax.ShapeDtypeStruct((rows, out), jnp.float32),
            jax.ShapeDtypeStruct((chips, rows, out), jnp.bfloat16),
        ),
        in_specs=[vmem] * 3,
        out_specs=(vmem,) * 2,
        compiler_params=pltpu.CompilerParams(vmem_limit_bytes=VMEM_LIMIT),
    )(parts, running, labels)


def per_device(size, center_feats, coeffs, labels, running, batch_index, landmark_index):
    chips = size // 2
    swap = [(i, i ^ 1) for i in range(size)]
    across = [[core + 2 * chip for chip in range(chips)] for core in range(2)]

    def exchange(blocks):
        return lax.all_to_all(
            blocks, "centers", 0, 0, axis_index_groups=across, tiled=True
        )

    picks = batch_index.shape[0]
    slab = center_feats.shape[0]
    own = gather_rows(center_feats, lax.rem(batch_index, slab), chips)
    mine = exchange(own).reshape(chips * picks, -1)
    other = lax.ppermute(mine, "centers", swap)
    tile, land_tile = kernel_tiles(
        mine, other, center_feats, lax.rem(landmark_index, slab)
    )
    pred_mine, pred_other = predictions(tile, coeffs.T)
    pair = pred_mine + lax.ppermute(pred_other, "centers", swap)
    parts = exchange(pair.reshape(chips, picks, -1))
    new_running, resid = residuals(parts, running, labels)
    resid_mine = exchange(resid).reshape(chips * picks, -1)
    resid_other = lax.ppermute(resid_mine, "centers", swap)
    projection = jnp.dot(
        land_tile,
        jnp.concatenate([resid_mine, resid_other], axis=0),
        preferred_element_type=jnp.float32,
    )
    return (new_running, projection)


def solution(mesh):
    row = P(("groups", "centers"), None)
    flat = P(("groups", "centers"))
    return jax.shard_map(
        functools.partial(per_device, mesh.shape["centers"]),
        mesh=mesh,
        in_specs=(row, row, row, row, flat, flat),
        out_specs=(row, row),
        check_vma=False,
    )
```

```python
import functools

import jax
import jax.numpy as jnp
from jax import lax
from jax.experimental import pallas as pl
from jax.experimental.pallas import tpu as pltpu
from jax.sharding import PartitionSpec as P

SCALE = 1024.0
SENT_SCALE = 128.0
VMEM_LIMIT = 16 * 1024 * 1024


def gather_kernel(index_ref, feats_ref, out_ref, rows):
    for i in range(index_ref.shape[0]):
        row = index_ref[i]
        start = pl.multiple_of((row // 16) * 16, 16)
        block = feats_ref[pl.ds(start, 16), :].astype(jnp.float32)
        here = lax.broadcasted_iota(jnp.int32, block.shape, 0) == row - start
        rows[i : i + 1, :] = jnp.sum(jnp.where(here, block, 0.0), axis=0, keepdims=True)
    picked = rows[...].astype(out_ref.dtype)
    for chip in range(out_ref.shape[0]):
        out_ref[chip] = picked


def gather_rows(center_feats, batch_index, chips):
    picks, width = batch_index.shape[0], center_feats.shape[1]
    vmem = pl.BlockSpec(memory_space=pltpu.VMEM)
    return pl.pallas_call(
        gather_kernel,
        out_shape=jax.ShapeDtypeStruct((chips, picks, width), center_feats.dtype),
        in_specs=[pl.BlockSpec(memory_space=pltpu.SMEM), vmem],
        out_specs=vmem,
        scratch_shapes=[pltpu.VMEM((picks, width), jnp.float32)],
        compiler_params=pltpu.CompilerParams(vmem_limit_bytes=VMEM_LIMIT),
    )(batch_index, center_feats)


def nt(a, b):
    return lax.dot_general(
        a, b, (((1,), (1,)), ((), ())), preferred_element_type=jnp.float32
    )


def tile_kernel(mine_ref, other_ref, feats_ref, land_ref, tile_ref, land_tile_ref):
    slab = feats_ref.shape[0]
    batch = jnp.concatenate([mine_ref[...], other_ref[...]], axis=0)
    feats = feats_ref[...]
    wide = feats.astype(jnp.float32)
    center_norms = jnp.sum(wide * wide, axis=1, keepdims=True)
    batch_wide = batch.astype(jnp.float32)
    batch_norms = jnp.sum(batch_wide * batch_wide, axis=1, keepdims=True)
    dist = center_norms + batch_norms.T - 2.0 * nt(feats, batch)
    tile = jnp.exp(-dist / SCALE).astype(jnp.bfloat16)
    tile_ref[...] = tile
    local = land_ref[...]
    chosen = lax.broadcasted_iota(jnp.int32, (local.shape[0], slab), 1) == local
    pick = jnp.where(chosen, 1.0, 0.0).astype(jnp.bfloat16)
    land_tile_ref[...] = jnp.dot(
        pick, tile, preferred_element_type=jnp.float32
    ).astype(jnp.bfloat16)


def kernel_tiles(mine, other, center_feats, land_local):
    half, lands, slab = mine.shape[0], land_local.shape[0], center_feats.shape[0]
    vmem = pl.BlockSpec(memory_space=pltpu.VMEM)
    return pl.pallas_call(
        tile_kernel,
        out_shape=(
            jax.ShapeDtypeStruct((slab, 2 * half), jnp.bfloat16),
            jax.ShapeDtypeStruct((lands, 2 * half), jnp.bfloat16),
        ),
        in_specs=[vmem] * 4,
        out_specs=(vmem,) * 2,
        compiler_params=pltpu.CompilerParams(
            vmem_limit_bytes=VMEM_LIMIT * (1 if half <= 64 else 3)
        ),
    )(mine, other, center_feats, land_local.reshape(lands, 1))


def pred_kernel(tile_ref, coeffs_ref, mine_ref, other_ref):
    pred = jnp.dot(
        coeffs_ref[...], tile_ref[...], preferred_element_type=jnp.float32
    ).T
    half = mine_ref.shape[0]
    mine_ref[...] = pred[:half]
    other_ref[...] = pred[half:]


def predictions(tile, coeffs_t):
    half, out = tile.shape[1] // 2, coeffs_t.shape[0]
    vmem = pl.BlockSpec(memory_space=pltpu.VMEM)
    return pl.pallas_call(
        pred_kernel,
        out_shape=(jax.ShapeDtypeStruct((half, out), jnp.float32),) * 2,
        in_specs=[vmem] * 2,
        out_specs=(vmem,) * 2,
        compiler_params=pltpu.CompilerParams(
            vmem_limit_bytes=VMEM_LIMIT * (1 if half <= 64 else 3)
        ),
    )(tile, coeffs_t)


def resid_kernel(parts_ref, running_ref, labels_ref, new_ref, resid_ref):
    total = running_ref[...]
    for chip in range(parts_ref.shape[0]):
        total = total + parts_ref[chip]
    new_ref[...] = total
    resid = (total - labels_ref[...].astype(jnp.float32)).astype(jnp.bfloat16)
    for chip in range(resid_ref.shape[0]):
        resid_ref[chip] = resid


def residuals(parts, running, labels):
    chips, rows, out = parts.shape
    vmem = pl.BlockSpec(memory_space=pltpu.VMEM)
    return pl.pallas_call(
        resid_kernel,
        out_shape=(
            jax.ShapeDtypeStruct((rows, out), jnp.float32),
            jax.ShapeDtypeStruct((chips, rows, out), jnp.bfloat16),
        ),
        in_specs=[vmem] * 3,
        out_specs=(vmem,) * 2,
        compiler_params=pltpu.CompilerParams(vmem_limit_bytes=VMEM_LIMIT),
    )(parts, running, labels)


def per_device(size, center_feats, coeffs, labels, running, batch_index, landmark_index):
    chips = size // 2
    swap = [(i, i ^ 1) for i in range(size)]
    across = [[core + 2 * chip for chip in range(chips)] for core in range(2)]

    def exchange(blocks):
        return lax.all_to_all(
            blocks, "centers", 0, 0, axis_index_groups=across, tiled=True
        )

    picks = batch_index.shape[0]
    slab = center_feats.shape[0]
    own = gather_rows(center_feats, lax.rem(batch_index, slab), chips)
    mine = exchange(own).reshape(chips * picks, -1)
    other = lax.ppermute(mine, "centers", swap)
    tile, land_tile = kernel_tiles(
        mine, other, center_feats, lax.rem(landmark_index, slab)
    )
    pred_mine, pred_other = predictions(tile, coeffs.T)
    pair = pred_mine + lax.ppermute(pred_other, "centers", swap)
    sent = (pair * SENT_SCALE).astype(jnp.float16)
    parts = exchange(sent.reshape(chips, picks, -1)).astype(jnp.float32)
    new_running = running + jnp.sum(parts, axis=0) / SENT_SCALE
    resid = (new_running - labels.astype(jnp.float32)).astype(jnp.bfloat16)
    resid = jnp.broadcast_to(resid, (chips,) + resid.shape)
    resid_mine = exchange(resid).reshape(chips * picks, -1)
    resid_other = lax.ppermute(resid_mine, "centers", swap)
    projection = jnp.dot(
        land_tile,
        jnp.concatenate([resid_mine, resid_other], axis=0),
        preferred_element_type=jnp.float32,
    )
    return (new_running, projection)


def solution(mesh):
    row = P(("groups", "centers"), None)
    flat = P(("groups", "centers"))
    return jax.shard_map(
        functools.partial(per_device, mesh.shape["centers"]),
        mesh=mesh,
        in_specs=(row, row, row, row, flat, flat),
        out_specs=(row, row),
        check_vma=False,
    )
```

```python
import functools

import jax
import jax.numpy as jnp
from jax import lax
from jax.experimental import pallas as pl
from jax.experimental.pallas import tpu as pltpu
from jax.sharding import PartitionSpec as P

SCALE = 1024.0
SENT_SCALE = 128.0
VMEM_LIMIT = 16 * 1024 * 1024


def vmem_limit(half):
    return pltpu.CompilerParams(vmem_limit_bytes=VMEM_LIMIT * (1 if half <= 64 else 3))


def local_kernel(slab, index_ref, out_ref):
    out_ref[...] = lax.rem(index_ref[...], slab)


def local_index(index, slab):
    vmem = pl.BlockSpec(memory_space=pltpu.VMEM)
    return pl.pallas_call(
        functools.partial(local_kernel, slab),
        out_shape=jax.ShapeDtypeStruct(index.shape, index.dtype),
        in_specs=[vmem],
        out_specs=vmem,
        compiler_params=pltpu.CompilerParams(vmem_limit_bytes=VMEM_LIMIT),
    )(index)


def gather_kernel(index_ref, feats_ref, out_ref, rows):
    for i in range(index_ref.shape[0]):
        row = index_ref[i]
        start = pl.multiple_of((row // 16) * 16, 16)
        block = feats_ref[pl.ds(start, 16), :].astype(jnp.float32)
        here = lax.broadcasted_iota(jnp.int32, block.shape, 0) == row - start
        rows[i : i + 1, :] = jnp.sum(jnp.where(here, block, 0.0), axis=0, keepdims=True)
    picked = rows[...].astype(out_ref.dtype)
    for chip in range(out_ref.shape[0]):
        out_ref[chip] = picked


def gather_rows(center_feats, batch_index, chips):
    picks, width = batch_index.shape[0], center_feats.shape[1]
    vmem = pl.BlockSpec(memory_space=pltpu.VMEM)
    return pl.pallas_call(
        gather_kernel,
        out_shape=jax.ShapeDtypeStruct((chips, picks, width), center_feats.dtype),
        in_specs=[pl.BlockSpec(memory_space=pltpu.SMEM), vmem],
        out_specs=vmem,
        scratch_shapes=[pltpu.VMEM((picks, width), jnp.float32)],
        compiler_params=pltpu.CompilerParams(vmem_limit_bytes=VMEM_LIMIT),
    )(batch_index, center_feats)


def nt(a, b):
    return lax.dot_general(
        a, b, (((1,), (1,)), ((), ())), preferred_element_type=jnp.float32
    )


def norm_kernel(mine_ref, feats_ref, centers_ref, mine_norms_ref):
    feats = feats_ref[...].astype(jnp.float32)
    centers_ref[...] = jnp.sum(feats * feats, axis=1, keepdims=True)
    mine = mine_ref[...].astype(jnp.float32)
    mine_norms_ref[...] = jnp.sum(mine * mine, axis=1, keepdims=True)


def norms(mine, center_feats):
    vmem = pl.BlockSpec(memory_space=pltpu.VMEM)
    return pl.pallas_call(
        norm_kernel,
        out_shape=(
            jax.ShapeDtypeStruct((center_feats.shape[0], 1), jnp.float32),
            jax.ShapeDtypeStruct((mine.shape[0], 1), jnp.float32),
        ),
        in_specs=[vmem] * 2,
        out_specs=(vmem,) * 2,
        compiler_params=vmem_limit(mine.shape[0]),
    )(mine, center_feats)


def tile_kernel(mine_ref, other_ref, feats_ref, centers_ref, mine_norms_ref, tile_ref):
    other = other_ref[...]
    batch = jnp.concatenate([mine_ref[...], other], axis=0)
    wide = other.astype(jnp.float32)
    other_norms = jnp.sum(wide * wide, axis=1, keepdims=True)
    batch_norms = jnp.concatenate([mine_norms_ref[...], other_norms], axis=0)
    dist = centers_ref[...] + batch_norms.T - 2.0 * nt(feats_ref[...], batch)
    tile_ref[...] = jnp.exp(-dist / SCALE).astype(jnp.bfloat16)


def kernel_tile(mine, other, center_feats, center_norms, mine_norms):
    half, slab = mine.shape[0], center_feats.shape[0]
    vmem = pl.BlockSpec(memory_space=pltpu.VMEM)
    return pl.pallas_call(
        tile_kernel,
        out_shape=jax.ShapeDtypeStruct((slab, 2 * half), jnp.bfloat16),
        in_specs=[vmem] * 5,
        out_specs=vmem,
        compiler_params=vmem_limit(half),
    )(mine, other, center_feats, center_norms, mine_norms)


def land_kernel(tile_ref, land_ref, land_tile_ref):
    tile = tile_ref[...]
    shape = (land_ref.shape[0], tile.shape[0])
    chosen = lax.broadcasted_iota(jnp.int32, shape, 1) == land_ref[...]
    pick = jnp.where(chosen, 1.0, 0.0).astype(jnp.bfloat16)
    land_tile_ref[...] = jnp.dot(
        pick, tile, preferred_element_type=jnp.float32
    ).astype(jnp.bfloat16)


def land_rows(tile, land_local):
    lands = land_local.shape[0]
    vmem = pl.BlockSpec(memory_space=pltpu.VMEM)
    return pl.pallas_call(
        land_kernel,
        out_shape=jax.ShapeDtypeStruct((lands, tile.shape[1]), jnp.bfloat16),
        in_specs=[vmem] * 2,
        out_specs=vmem,
        compiler_params=vmem_limit(tile.shape[1] // 2),
    )(tile, land_local.reshape(lands, 1))


def pred_kernel(tile_ref, coeffs_ref, mine_ref, other_ref):
    pred = jnp.dot(
        coeffs_ref[...], tile_ref[...], preferred_element_type=jnp.float32
    ).T
    half = mine_ref.shape[0]
    mine_ref[...] = pred[:half]
    other_ref[...] = pred[half:]


def predictions(tile, coeffs_t):
    half, out = tile.shape[1] // 2, coeffs_t.shape[0]
    vmem = pl.BlockSpec(memory_space=pltpu.VMEM)
    return pl.pallas_call(
        pred_kernel,
        out_shape=(jax.ShapeDtypeStruct((half, out), jnp.float32),) * 2,
        in_specs=[vmem] * 2,
        out_specs=(vmem,) * 2,
        compiler_params=vmem_limit(half),
    )(tile, coeffs_t)


def per_device(size, center_feats, coeffs, labels, running, batch_index, landmark_index):
    chips = size // 2
    swap = [(i, i ^ 1) for i in range(size)]
    across = [[2 * chip + (chip.bit_count() + core) % 2 for chip in range(chips)] for core in range(2)]

    def exchange(blocks):
        return lax.all_to_all(
            blocks, "centers", 0, 0, axis_index_groups=across, tiled=True
        )

    picks = batch_index.shape[0]
    slab = center_feats.shape[0]
    own = gather_rows(center_feats, local_index(batch_index, slab), chips)
    mine = exchange(own).reshape(chips * picks, -1)
    other = lax.ppermute(mine, "centers", swap)
    center_norms, mine_norms = norms(mine, center_feats)
    tile = kernel_tile(mine, other, center_feats, center_norms, mine_norms)
    pred_mine, pred_other = predictions(tile, coeffs.T)
    land_tile = land_rows(tile, lax.rem(landmark_index, slab))
    pair = pred_mine + lax.ppermute(pred_other, "centers", swap)
    sent = (pair * SENT_SCALE).astype(jnp.float16)
    parts = exchange(sent.reshape(chips, picks, -1)).astype(jnp.float32)
    new_running = running + jnp.sum(parts, axis=0) / SENT_SCALE
    resid = (new_running - labels.astype(jnp.float32)).astype(jnp.bfloat16)
    resid = jnp.broadcast_to(resid, (chips,) + resid.shape)
    resid_mine = exchange(resid).reshape(chips * picks, -1)
    resid_other = lax.ppermute(resid_mine, "centers", swap)
    projection = jnp.dot(
        land_tile,
        jnp.concatenate([resid_mine, resid_other], axis=0),
        preferred_element_type=jnp.float32,
    )
    return (new_running, projection)


def solution(mesh):
    row = P(("groups", "centers"), None)
    flat = P(("groups", "centers"))
    return jax.shard_map(
        functools.partial(per_device, mesh.shape["centers"]),
        mesh=mesh,
        in_specs=(row, row, row, row, flat, flat),
        out_specs=(row, row),
        check_vma=False,
    )
```

```python
import functools

import jax
import jax.numpy as jnp
from jax import lax
from jax.experimental import pallas as pl
from jax.experimental.pallas import tpu as pltpu
from jax.sharding import PartitionSpec as P

SCALE = 1024.0
SENT_SCALE = 128.0
LONG = 10**10
VMEM_LIMIT = 16 * 1024 * 1024


def vmem_limit(half):
    return pltpu.CompilerParams(vmem_limit_bytes=VMEM_LIMIT * (1 if half <= 64 else 3))


def local_kernel(slab, index_ref, out_ref):
    out_ref[...] = lax.rem(index_ref[...], slab)


def local_index(index, slab):
    vmem = pl.BlockSpec(memory_space=pltpu.VMEM)
    return pl.pallas_call(
        functools.partial(local_kernel, slab),
        out_shape=jax.ShapeDtypeStruct(index.shape, index.dtype),
        in_specs=[vmem],
        out_specs=vmem,
        compiler_params=pltpu.CompilerParams(vmem_limit_bytes=VMEM_LIMIT),
        cost_estimate=pl.CostEstimate(flops=LONG, bytes_accessed=0, transcendentals=0),
    )(index)


def gather_kernel(index_ref, feats_ref, out_ref, rows):
    for i in range(index_ref.shape[0]):
        row = index_ref[i]
        start = pl.multiple_of((row // 16) * 16, 16)
        block = feats_ref[pl.ds(start, 16), :].astype(jnp.float32)
        here = lax.broadcasted_iota(jnp.int32, block.shape, 0) == row - start
        rows[i : i + 1, :] = jnp.sum(jnp.where(here, block, 0.0), axis=0, keepdims=True)
    picked = rows[...].astype(out_ref.dtype)
    for chip in range(out_ref.shape[0]):
        out_ref[chip] = picked


def gather_rows(center_feats, batch_index, chips):
    picks, width = batch_index.shape[0], center_feats.shape[1]
    vmem = pl.BlockSpec(memory_space=pltpu.VMEM)
    return pl.pallas_call(
        gather_kernel,
        out_shape=jax.ShapeDtypeStruct((chips, picks, width), center_feats.dtype),
        in_specs=[pl.BlockSpec(memory_space=pltpu.SMEM), vmem],
        out_specs=vmem,
        scratch_shapes=[pltpu.VMEM((picks, width), jnp.float32)],
        compiler_params=pltpu.CompilerParams(vmem_limit_bytes=VMEM_LIMIT),
    )(batch_index, center_feats)


def nt(a, b):
    return lax.dot_general(
        a, b, (((1,), (1,)), ((), ())), preferred_element_type=jnp.float32
    )


def norm_kernel(mine_ref, feats_ref, centers_ref, mine_norms_ref):
    feats = feats_ref[...].astype(jnp.float32)
    centers_ref[...] = jnp.sum(feats * feats, axis=1, keepdims=True)
    mine = mine_ref[...].astype(jnp.float32)
    mine_norms_ref[...] = jnp.sum(mine * mine, axis=1, keepdims=True)


def norms(mine, center_feats):
    vmem = pl.BlockSpec(memory_space=pltpu.VMEM)
    return pl.pallas_call(
        norm_kernel,
        out_shape=(
            jax.ShapeDtypeStruct((center_feats.shape[0], 1), jnp.float32),
            jax.ShapeDtypeStruct((mine.shape[0], 1), jnp.float32),
        ),
        in_specs=[vmem] * 2,
        out_specs=(vmem,) * 2,
        compiler_params=vmem_limit(mine.shape[0]),
    )(mine, center_feats)


def tile_kernel(mine_ref, other_ref, feats_ref, centers_ref, mine_norms_ref, tile_ref):
    other = other_ref[...]
    batch = jnp.concatenate([mine_ref[...], other], axis=0)
    wide = other.astype(jnp.float32)
    other_norms = jnp.sum(wide * wide, axis=1, keepdims=True)
    batch_norms = jnp.concatenate([mine_norms_ref[...], other_norms], axis=0)
    dist = centers_ref[...] + batch_norms.T - 2.0 * nt(feats_ref[...], batch)
    tile_ref[...] = jnp.exp(-dist / SCALE).astype(jnp.bfloat16)


def kernel_tile(mine, other, center_feats, center_norms, mine_norms):
    half, slab = mine.shape[0], center_feats.shape[0]
    vmem = pl.BlockSpec(memory_space=pltpu.VMEM)
    return pl.pallas_call(
        tile_kernel,
        out_shape=jax.ShapeDtypeStruct((slab, 2 * half), jnp.bfloat16),
        in_specs=[vmem] * 5,
        out_specs=vmem,
        compiler_params=vmem_limit(half),
    )(mine, other, center_feats, center_norms, mine_norms)


def land_kernel(tile_ref, land_ref, land_tile_ref):
    tile = tile_ref[...]
    shape = (land_ref.shape[0], tile.shape[0])
    chosen = lax.broadcasted_iota(jnp.int32, shape, 1) == land_ref[...]
    pick = jnp.where(chosen, 1.0, 0.0).astype(jnp.bfloat16)
    land_tile_ref[...] = jnp.dot(
        pick, tile, preferred_element_type=jnp.float32
    ).astype(jnp.bfloat16)


def land_rows(tile, land_local):
    lands = land_local.shape[0]
    vmem = pl.BlockSpec(memory_space=pltpu.VMEM)
    return pl.pallas_call(
        land_kernel,
        out_shape=jax.ShapeDtypeStruct((lands, tile.shape[1]), jnp.bfloat16),
        in_specs=[vmem] * 2,
        out_specs=vmem,
        compiler_params=vmem_limit(tile.shape[1] // 2),
    )(tile, land_local.reshape(lands, 1))


def pred_kernel(tile_ref, coeffs_ref, mine_ref, other_ref):
    pred = jnp.dot(
        coeffs_ref[...], tile_ref[...], preferred_element_type=jnp.float32
    ).T
    half = mine_ref.shape[0]
    mine_ref[...] = pred[:half]
    other_ref[...] = pred[half:]


def predictions(tile, coeffs_t):
    half, out = tile.shape[1] // 2, coeffs_t.shape[0]
    vmem = pl.BlockSpec(memory_space=pltpu.VMEM)
    return pl.pallas_call(
        pred_kernel,
        out_shape=(jax.ShapeDtypeStruct((half, out), jnp.float32),) * 2,
        in_specs=[vmem] * 2,
        out_specs=(vmem,) * 2,
        compiler_params=vmem_limit(half),
    )(tile, coeffs_t)


def per_device(size, center_feats, coeffs, labels, running, batch_index, landmark_index):
    chips = size // 2
    swap = [(i, i ^ 1) for i in range(size)]
    across = [[2 * chip + (chip.bit_count() + core) % 2 for chip in range(chips)] for core in range(2)]

    def exchange(blocks):
        return lax.all_to_all(
            blocks, "centers", 0, 0, axis_index_groups=across, tiled=True
        )

    picks = batch_index.shape[0]
    slab = center_feats.shape[0]
    own = gather_rows(center_feats, local_index(batch_index, slab), chips)
    mine = exchange(own).reshape(chips * picks, -1)
    other = lax.ppermute(mine, "centers", swap)
    center_norms, mine_norms = norms(mine, center_feats)
    tile = kernel_tile(mine, other, center_feats, center_norms, mine_norms)
    pred_mine, pred_other = predictions(tile, coeffs.T)
    land_tile = land_rows(tile, lax.rem(landmark_index, slab))
    pair = pred_mine + lax.ppermute(pred_other, "centers", swap)
    sent = (pair * SENT_SCALE).astype(jnp.float16)
    parts = exchange(sent.reshape(chips, picks, -1)).astype(jnp.float32)
    new_running = running + jnp.sum(parts, axis=0) / SENT_SCALE
    resid = (new_running - labels.astype(jnp.float32)).astype(jnp.bfloat16)
    resid = jnp.broadcast_to(resid, (chips,) + resid.shape)
    resid_mine = exchange(resid).reshape(chips * picks, -1)
    resid_other = lax.ppermute(resid_mine, "centers", swap)
    projection = jnp.dot(
        land_tile,
        jnp.concatenate([resid_mine, resid_other], axis=0),
        preferred_element_type=jnp.float32,
    )
    return (new_running, projection)


def solution(mesh):
    row = P(("groups", "centers"), None)
    flat = P(("groups", "centers"))
    return jax.shard_map(
        functools.partial(per_device, mesh.shape["centers"]),
        mesh=mesh,
        in_specs=(row, row, row, row, flat, flat),
        out_specs=(row, row),
        check_vma=False,
    )
```

```python
import functools

import jax
import jax.numpy as jnp
from jax import lax
from jax.experimental import pallas as pl
from jax.experimental.pallas import tpu as pltpu
from jax.sharding import PartitionSpec as P

SCALE = 1024.0
SENT_SCALE = 128.0
LONG = 10**10
VMEM_LIMIT = 16 * 1024 * 1024


def vmem_limit(half):
    return pltpu.CompilerParams(vmem_limit_bytes=VMEM_LIMIT * (1 if half <= 64 else 3))


def local_kernel(slab, index_ref, out_ref):
    out_ref[...] = lax.rem(index_ref[...], slab)


def local_index(index, slab):
    vmem = pl.BlockSpec(memory_space=pltpu.VMEM)
    return pl.pallas_call(
        functools.partial(local_kernel, slab),
        out_shape=jax.ShapeDtypeStruct(index.shape, index.dtype),
        in_specs=[vmem],
        out_specs=vmem,
        compiler_params=pltpu.CompilerParams(vmem_limit_bytes=VMEM_LIMIT),
        cost_estimate=pl.CostEstimate(flops=LONG, bytes_accessed=0, transcendentals=0),
    )(index)


def gather_kernel(index_ref, feats_ref, out_ref, rows):
    for i in range(index_ref.shape[0]):
        row = index_ref[i]
        start = pl.multiple_of((row // 16) * 16, 16)
        block = feats_ref[pl.ds(start, 16), :].astype(jnp.float32)
        here = lax.broadcasted_iota(jnp.int32, block.shape, 0) == row - start
        rows[i : i + 1, :] = jnp.sum(jnp.where(here, block, 0.0), axis=0, keepdims=True)
    picked = rows[...].astype(out_ref.dtype)
    for chip in range(out_ref.shape[0]):
        out_ref[chip] = picked


def gather_rows(center_feats, batch_index, chips):
    picks, width = batch_index.shape[0], center_feats.shape[1]
    vmem = pl.BlockSpec(memory_space=pltpu.VMEM)
    return pl.pallas_call(
        gather_kernel,
        out_shape=jax.ShapeDtypeStruct((chips, picks, width), center_feats.dtype),
        in_specs=[pl.BlockSpec(memory_space=pltpu.SMEM), vmem],
        out_specs=vmem,
        scratch_shapes=[pltpu.VMEM((picks, width), jnp.float32)],
        compiler_params=pltpu.CompilerParams(vmem_limit_bytes=VMEM_LIMIT),
    )(batch_index, center_feats)


def nt(a, b):
    return lax.dot_general(
        a, b, (((1,), (1,)), ((), ())), preferred_element_type=jnp.float32
    )


def norm_kernel(mine_ref, feats_ref, centers_ref, mine_norms_ref):
    feats = feats_ref[...].astype(jnp.float32)
    centers_ref[...] = jnp.sum(feats * feats, axis=1, keepdims=True)
    mine = mine_ref[...].astype(jnp.float32)
    mine_norms_ref[...] = jnp.sum(mine * mine, axis=1, keepdims=True)


def norms(mine, center_feats):
    vmem = pl.BlockSpec(memory_space=pltpu.VMEM)
    return pl.pallas_call(
        norm_kernel,
        out_shape=(
            jax.ShapeDtypeStruct((center_feats.shape[0], 1), jnp.float32),
            jax.ShapeDtypeStruct((mine.shape[0], 1), jnp.float32),
        ),
        in_specs=[vmem] * 2,
        out_specs=(vmem,) * 2,
        compiler_params=vmem_limit(mine.shape[0]),
    )(mine, center_feats)


def tile_kernel(mine_ref, other_ref, feats_ref, centers_ref, mine_norms_ref, tile_ref):
    other = other_ref[...]
    batch = jnp.concatenate([mine_ref[...], other], axis=0)
    wide = other.astype(jnp.float32)
    other_norms = jnp.sum(wide * wide, axis=1, keepdims=True)
    batch_norms = jnp.concatenate([mine_norms_ref[...], other_norms], axis=0)
    dist = centers_ref[...] + batch_norms.T - 2.0 * nt(feats_ref[...], batch)
    tile_ref[...] = jnp.exp(-dist / SCALE).astype(jnp.bfloat16)


def kernel_tile(mine, other, center_feats, center_norms, mine_norms):
    half, slab = mine.shape[0], center_feats.shape[0]
    vmem = pl.BlockSpec(memory_space=pltpu.VMEM)
    return pl.pallas_call(
        tile_kernel,
        out_shape=jax.ShapeDtypeStruct((slab, 2 * half), jnp.bfloat16),
        in_specs=[vmem] * 5,
        out_specs=vmem,
        compiler_params=vmem_limit(half),
    )(mine, other, center_feats, center_norms, mine_norms)


def land_kernel(tile_ref, land_ref, land_tile_ref):
    tile = tile_ref[...]
    shape = (land_ref.shape[0], tile.shape[0])
    chosen = lax.broadcasted_iota(jnp.int32, shape, 1) == land_ref[...]
    pick = jnp.where(chosen, 1.0, 0.0).astype(jnp.bfloat16)
    land_tile_ref[...] = jnp.dot(
        pick, tile, preferred_element_type=jnp.float32
    ).astype(jnp.bfloat16)


def land_rows(tile, land_local):
    lands = land_local.shape[0]
    vmem = pl.BlockSpec(memory_space=pltpu.VMEM)
    return pl.pallas_call(
        land_kernel,
        out_shape=jax.ShapeDtypeStruct((lands, tile.shape[1]), jnp.bfloat16),
        in_specs=[vmem] * 2,
        out_specs=vmem,
        compiler_params=vmem_limit(tile.shape[1] // 2),
    )(tile, land_local.reshape(lands, 1))


def pred_kernel(tile_ref, coeffs_ref, mine_ref, other_ref):
    pred = jnp.dot(
        coeffs_ref[...], tile_ref[...], preferred_element_type=jnp.float32
    ).T
    half = mine_ref.shape[0]
    mine_ref[...] = pred[:half]
    other_ref[...] = pred[half:]


def predictions(tile, coeffs_t):
    half, out = tile.shape[1] // 2, coeffs_t.shape[0]
    vmem = pl.BlockSpec(memory_space=pltpu.VMEM)
    return pl.pallas_call(
        pred_kernel,
        out_shape=(jax.ShapeDtypeStruct((half, out), jnp.float32),) * 2,
        in_specs=[vmem] * 2,
        out_specs=(vmem,) * 2,
        compiler_params=vmem_limit(half),
    )(tile, coeffs_t)


def per_device(size, center_feats, coeffs, labels, running, batch_index, landmark_index):
    chips = size // 2
    swap = [(i, i ^ 1) for i in range(size)]
    across = [[2 * chip + (chip.bit_count() + core) % 2 for chip in range(chips)] for core in range(2)]

    def exchange(blocks):
        return lax.all_to_all(
            blocks, "centers", 0, 0, axis_index_groups=across, tiled=True
        )

    picks = batch_index.shape[0]
    slab = center_feats.shape[0]
    own = gather_rows(center_feats, local_index(batch_index, slab), chips)
    mine = exchange(own).reshape(chips * picks, -1)
    other = lax.ppermute(mine, "centers", swap)
    center_norms, mine_norms = norms(mine, center_feats)
    tile = kernel_tile(mine, other, center_feats, center_norms, mine_norms)
    pred_mine, pred_other = predictions(tile, coeffs.T)
    land_tile = land_rows(tile, lax.rem(landmark_index, slab))
    crossed = lax.ppermute(
        (pred_other * SENT_SCALE).astype(jnp.float16), "centers", swap
    )
    sent = (pred_mine * SENT_SCALE + crossed.astype(jnp.float32)).astype(jnp.float16)
    parts = exchange(sent.reshape(chips, picks, -1)).astype(jnp.float32)
    new_running = running + jnp.sum(parts, axis=0) / SENT_SCALE
    resid = (new_running - labels.astype(jnp.float32)).astype(jnp.bfloat16)
    resid = jnp.broadcast_to(resid, (chips,) + resid.shape)
    resid_mine = exchange(resid).reshape(chips * picks, -1)
    resid_other = lax.ppermute(resid_mine, "centers", swap)
    projection = jnp.dot(
        land_tile,
        jnp.concatenate([resid_mine, resid_other], axis=0),
        preferred_element_type=jnp.float32,
    )
    return (new_running, projection)


def solution(mesh):
    row = P(("groups", "centers"), None)
    flat = P(("groups", "centers"))
    return jax.shard_map(
        functools.partial(per_device, mesh.shape["centers"]),
        mesh=mesh,
        in_specs=(row, row, row, row, flat, flat),
        out_specs=(row, row),
        check_vma=False,
    )
```

```python
import functools

import jax
import jax.numpy as jnp
from jax import lax
from jax.experimental import pallas as pl
from jax.experimental.pallas import tpu as pltpu
from jax.sharding import PartitionSpec as P

SCALE = 1024.0
SENT_SCALE = 128.0
LONG = 10**10
VMEM_LIMIT = 16 * 1024 * 1024


def vmem_limit(half):
    return pltpu.CompilerParams(vmem_limit_bytes=VMEM_LIMIT * (1 if half <= 64 else 3))


def local_kernel(slab, index_ref, out_ref):
    out_ref[...] = lax.rem(index_ref[...], slab)


def local_index(index, slab):
    vmem = pl.BlockSpec(memory_space=pltpu.VMEM)
    return pl.pallas_call(
        functools.partial(local_kernel, slab),
        out_shape=jax.ShapeDtypeStruct(index.shape, index.dtype),
        in_specs=[vmem],
        out_specs=vmem,
        compiler_params=pltpu.CompilerParams(vmem_limit_bytes=VMEM_LIMIT),
        cost_estimate=pl.CostEstimate(flops=LONG, bytes_accessed=0, transcendentals=0),
    )(index)


def gather_kernel(index_ref, feats_ref, out_ref, rows):
    for i in range(index_ref.shape[0]):
        row = index_ref[i]
        start = pl.multiple_of((row // 16) * 16, 16)
        block = feats_ref[pl.ds(start, 16), :].astype(jnp.float32)
        here = lax.broadcasted_iota(jnp.int32, block.shape, 0) == row - start
        rows[i : i + 1, :] = jnp.sum(jnp.where(here, block, 0.0), axis=0, keepdims=True)
    picked = rows[...].astype(out_ref.dtype)
    for chip in range(out_ref.shape[0]):
        out_ref[chip] = picked


def gather_rows(center_feats, batch_index, chips):
    picks, width = batch_index.shape[0], center_feats.shape[1]
    vmem = pl.BlockSpec(memory_space=pltpu.VMEM)
    return pl.pallas_call(
        gather_kernel,
        out_shape=jax.ShapeDtypeStruct((chips, picks, width), center_feats.dtype),
        in_specs=[pl.BlockSpec(memory_space=pltpu.SMEM), vmem],
        out_specs=vmem,
        scratch_shapes=[pltpu.VMEM((picks, width), jnp.float32)],
        compiler_params=pltpu.CompilerParams(vmem_limit_bytes=VMEM_LIMIT),
    )(batch_index, center_feats)


def nt(a, b):
    return lax.dot_general(
        a, b, (((1,), (1,)), ((), ())), preferred_element_type=jnp.float32
    )


def norm_kernel(mine_ref, feats_ref, centers_ref, mine_norms_ref):
    feats = feats_ref[...].astype(jnp.float32)
    centers_ref[...] = jnp.sum(feats * feats, axis=1, keepdims=True)
    mine = mine_ref[...].astype(jnp.float32)
    mine_norms_ref[...] = jnp.sum(mine * mine, axis=1, keepdims=True)


def norms(mine, center_feats):
    vmem = pl.BlockSpec(memory_space=pltpu.VMEM)
    return pl.pallas_call(
        norm_kernel,
        out_shape=(
            jax.ShapeDtypeStruct((center_feats.shape[0], 1), jnp.float32),
            jax.ShapeDtypeStruct((mine.shape[0], 1), jnp.float32),
        ),
        in_specs=[vmem] * 2,
        out_specs=(vmem,) * 2,
        compiler_params=vmem_limit(mine.shape[0]),
    )(mine, center_feats)


def tile_kernel(mine_ref, other_ref, feats_ref, centers_ref, mine_norms_ref, tile_ref):
    other = other_ref[...]
    batch = jnp.concatenate([mine_ref[...], other], axis=0)
    wide = other.astype(jnp.float32)
    other_norms = jnp.sum(wide * wide, axis=1, keepdims=True)
    batch_norms = jnp.concatenate([mine_norms_ref[...], other_norms], axis=0)
    dist = centers_ref[...] + batch_norms.T - 2.0 * nt(feats_ref[...], batch)
    tile_ref[...] = jnp.exp(-dist / SCALE).astype(jnp.bfloat16)


def kernel_tile(mine, other, center_feats, center_norms, mine_norms):
    half, slab = mine.shape[0], center_feats.shape[0]
    vmem = pl.BlockSpec(memory_space=pltpu.VMEM)
    return pl.pallas_call(
        tile_kernel,
        out_shape=jax.ShapeDtypeStruct((slab, 2 * half), jnp.bfloat16),
        in_specs=[vmem] * 5,
        out_specs=vmem,
        compiler_params=vmem_limit(half),
    )(mine, other, center_feats, center_norms, mine_norms)


def land_kernel(tile_ref, land_ref, land_tile_ref):
    tile = tile_ref[...]
    shape = (land_ref.shape[0], tile.shape[0])
    chosen = lax.broadcasted_iota(jnp.int32, shape, 1) == land_ref[...]
    pick = jnp.where(chosen, 1.0, 0.0).astype(jnp.bfloat16)
    land_tile_ref[...] = jnp.dot(
        pick, tile, preferred_element_type=jnp.float32
    ).astype(jnp.bfloat16)


def land_rows(tile, land_local):
    lands = land_local.shape[0]
    vmem = pl.BlockSpec(memory_space=pltpu.VMEM)
    return pl.pallas_call(
        land_kernel,
        out_shape=jax.ShapeDtypeStruct((lands, tile.shape[1]), jnp.bfloat16),
        in_specs=[vmem] * 2,
        out_specs=vmem,
        compiler_params=vmem_limit(tile.shape[1] // 2),
    )(tile, land_local.reshape(lands, 1))


def pred_kernel(tile_ref, coeffs_ref, mine_ref, other_ref):
    pred = jnp.dot(
        coeffs_ref[...], tile_ref[...], preferred_element_type=jnp.float32
    ).T
    half = mine_ref.shape[0]
    mine_ref[...] = pred[:half]
    other_ref[...] = pred[half:]


def predictions(tile, coeffs_t):
    half, out = tile.shape[1] // 2, coeffs_t.shape[0]
    vmem = pl.BlockSpec(memory_space=pltpu.VMEM)
    return pl.pallas_call(
        pred_kernel,
        out_shape=(jax.ShapeDtypeStruct((half, out), jnp.float32),) * 2,
        in_specs=[vmem] * 2,
        out_specs=(vmem,) * 2,
        compiler_params=vmem_limit(half),
    )(tile, coeffs_t)


def per_device(size, center_feats, coeffs, labels, running, batch_index, landmark_index):
    chips = size // 2
    swap = [(i, i ^ 1) for i in range(size)]
    across = [[2 * chip + (chip.bit_count() + core) % 2 for chip in range(chips)] for core in range(2)]

    def exchange(blocks):
        return lax.all_to_all(
            blocks, "centers", 0, 0, axis_index_groups=across, tiled=True
        )

    picks = batch_index.shape[0]
    slab = center_feats.shape[0]
    own = gather_rows(center_feats, local_index(batch_index, slab), chips)
    mine = exchange(own).reshape(chips * picks, -1)
    other = lax.ppermute(mine, "centers", swap)
    center_norms, mine_norms = norms(mine, center_feats)
    tile = kernel_tile(mine, other, center_feats, center_norms, mine_norms)
    pred_mine, pred_other = predictions(tile, coeffs.T)
    land_tile = land_rows(tile, lax.rem(landmark_index, slab))
    crossed = lax.ppermute(
        (pred_other * SENT_SCALE).astype(jnp.float16), "centers", swap
    )
    sent = (pred_mine * SENT_SCALE + crossed.astype(jnp.float32)).astype(jnp.float16)
    parts = exchange(sent.reshape(chips, picks, -1))

    def updated(running, parts):
        return running + jnp.sum(parts.astype(jnp.float32), axis=0) / SENT_SCALE

    resid = updated(running, parts) - labels.astype(jnp.float32)
    resid = resid.astype(jnp.bfloat16)
    resid = jnp.broadcast_to(resid, (chips,) + resid.shape)
    resid_mine = exchange(resid).reshape(chips * picks, -1)
    later_running, later_parts, resid_mine = lax.optimization_barrier(
        (running, parts, resid_mine)
    )
    new_running = updated(later_running, later_parts)
    resid_other = lax.ppermute(resid_mine, "centers", swap)
    projection = jnp.dot(
        land_tile,
        jnp.concatenate([resid_mine, resid_other], axis=0),
        preferred_element_type=jnp.float32,
    )
    return (new_running, projection)


def solution(mesh):
    row = P(("groups", "centers"), None)
    flat = P(("groups", "centers"))
    return jax.shard_map(
        functools.partial(per_device, mesh.shape["centers"]),
        mesh=mesh,
        in_specs=(row, row, row, row, flat, flat),
        out_specs=(row, row),
        check_vma=False,
    )
```
